32 devices in a mesh: group: 2 (over x), row: 16 (over z, y, core).
Axes of the slice: x: 2, y: 2, z: 4, core: 2. Of those that a mesh axis runs over, the one named last changes fastest.
Arguments:
- sources: float32 [4, 16, 8192], P('group', None, 'row'), parts along dimension 0, may hold values from -6 to 6
- lower_sources: float32 [4, 16, 8192], P('group', None, 'row'), parts along dimension 0, may hold values from -6 to 6
- upper_operator: float32 [16384, 8192], P(('group', 'row')), parts along dimension 0, may hold values from -0.0625 to 0.0625
- lower_operator: float32 [16384, 8192], P(('group', 'row')), parts along dimension 0, may hold values from -0.0625 to 0.0625
- upper_impedance: float32 [16384], P(('group', 'row')), parts along dimension 0, may hold values from 0.5 to 2
- lower_impedance: float32 [16384], P(('group', 'row')), parts along dimension 0, may hold values from 0.5 to 2
Outputs:
- lower_field: float32 [4, 16, 8192], P('group', None, 'row'), parts along dimension 0
- reflected: float32 [4, 16, 8192], P('group', None, 'row'), parts along dimension 0
The draws below stay inside these ranges and needn't reach their ends.
There are 2 independent parts, one for each index of `group`. The reference program is written for one: setup_inputs(seed, part) draws one part's arguments, and reference() takes and returns one part's arrays. A program takes and returns all parts, laid end to end along the dimension named above; each array names one. Nothing has to cross between parts.
All inputs are finite; a program needn't handle non-finite values.
Results may differ from the reference program's by a relative error of at most 0.000098.
Values sent between devices are 32-bit elements; how exact they have to be, the bound alone decides.
A program may use at most 64 MiB of HBM per device.

```python
import math
import jax
import jax.numpy as jnp
from jax import lax

N = 8192
COLS = 16
BATCHES = 2


def level_of(key, extent, cuts, smallest, largest):
    gain, own = 1.0, jax.random.fold_in(key, 6)
    for dim, shards_of in cuts:
        heights = jnp.exp(jax.random.uniform(jax.random.fold_in(own, dim), (shards_of,), jnp.float32, smallest / len(cuts), largest / len(cuts)))
        gain = gain * jnp.repeat(heights, extent[dim] // shards_of).reshape([-1 if axis == dim else 1 for axis in range(len(extent))])
    return gain


def gaussian(stream_key, shape, scale, reach, cuts=(), kind=jnp.bfloat16):
    gain = level_of(stream_key, shape, cuts, -0.22, 0.18) if cuts else 1.0
    result = jax.random.normal(stream_key, shape, jnp.float32) * scale * gain
    return jnp.minimum(jnp.maximum(result, -reach), reach).astype(kind)


def setup_inputs(seed: int = 0, part: int = 0) -> dict:
    seeds = jax.random.split(jax.random.key(seed), 7)
    part_keys = jax.random.split(jax.random.fold_in(seeds[6], part), 7)
    return {
        "sources": gaussian(part_keys[0], (BATCHES, COLS, N), 1.0, 6.0, ((2, 16),), jnp.float32),
        "lower_sources": gaussian(part_keys[1], (BATCHES, COLS, N), 1.0, 6.0, ((2, 16),), jnp.float32),
        "upper_operator": gaussian(part_keys[2], (N, N), N ** -0.5, 0.0625, ((0, 16),), jnp.float32),
        "lower_operator": gaussian(part_keys[3], (N, N), N ** -0.5, 0.0625, ((0, 16),), jnp.float32),
        "upper_impedance": jnp.clip(jnp.exp(math.log(2.0) - 1.3862944 * jax.random.uniform(part_keys[4], (N,), jnp.float32) ** level_of(part_keys[4], (N,), ((0, 16),), -0.2, 0.2)), 0.5, 2.0),
        "lower_impedance": jnp.clip(jnp.exp(math.log(2.0) - 1.3862944 * jax.random.uniform(part_keys[5], (N,), jnp.float32) ** level_of(part_keys[5], (N,), ((0, 16),), -0.2, 0.2)), 0.5, 2.0),
    }


def reference(sources, lower_sources, upper_operator, lower_operator, upper_impedance, lower_impedance):
    highest = lax.Precision.HIGHEST
    downward = jnp.einsum("bcj,ij->bci", sources, upper_operator, precision=highest)
    lower_field = jnp.einsum("bcj,ij->bci", downward, lower_operator, precision=highest)
    scaled = lower_impedance * lower_field + lower_sources
    bounced = jnp.einsum("bci,ij->bcj", scaled, lower_operator, precision=highest)
    mixed = upper_impedance * bounced - downward
    reflected = jnp.einsum("bci,ij->bcj", mixed, upper_operator, precision=highest)
    return lower_field, reflected
```

```python
import functools

import jax
import jax.numpy as jnp
from jax import lax
from jax.experimental import pallas as pl
from jax.experimental.pallas import tpu as pltpu
from jax.sharding import PartitionSpec as P

MESH = pl.DeviceIdType.MESH
F32, BF16 = jnp.float32, jnp.bfloat16
NT = (((1,), (1,)), ((), ()))
NN = (((1,), (0,)), ((), ()))


def split(value):
    high = value.astype(BF16)
    return high, (value - high.astype(F32)).astype(BF16)


def stacked(value):
    high, low = split(value)
    return jnp.concatenate([high, low], axis=0), high


def product(both, high, operator_high, operator_low, dims):
    rows = high.shape[0]
    main = lax.dot_general(both, operator_high, dims, preferred_element_type=F32)
    rest = lax.dot_general(high, operator_low, dims, preferred_element_type=F32)
    return main[:rows] + main[rows:] + rest


def kernel(lines, sides, cores, source_ref, inside_ref, upper_hbm, lower_hbm, upper_gain, lower_gain,
           field_ref, reflected_ref,
           stage, upper_high, upper_low, lower_high, lower_low, gathered, down_ref,
           core_out, core_in, side_out, side_in, line_out, line_in,
           load_sem, gather_send, gather_recv, core_send, core_recv, side_send, side_recv, line_send, line_recv):
    size = source_ref.shape[1]
    me = lax.axis_index("row")
    core = lax.rem(me, cores)
    side = lax.rem(me // cores, sides)
    line = me // (cores * sides)

    def at(dz, dy, dc):
        return (lax.rem(line + dz, lines) * sides + lax.rem(side + dy, sides)) * cores + lax.rem(core + dc, cores)

    def slot_of(dz, dy, dc):
        return (dz * sides + dy) * cores + dc

    slots = [(dz, dy, dc) for dz in range(lines) for dy in range(sides) for dc in range(cores)]

    def load(operator, which, key):
        slot = slot_of(*key)
        columns = pl.ds(pl.multiple_of(at(*key) * size, size), size)
        copy = pltpu.make_async_copy(operator.at[:, columns], stage.at[slot], load_sem.at[which, slot])
        copy.start()
        return copy

    upper_loads = [load(upper_hbm, 0, key) for key in slots]

    partners = [at(0, 0, 1), at(0, 1, 0)] + [at(dz, 0, 0) for dz in range(1, lines)]
    barrier = pltpu.get_barrier_semaphore()
    for partner in partners:
        pl.semaphore_signal(barrier, inc=1, device_id={"row": partner}, device_id_type=MESH)
    pl.semaphore_wait(barrier, len(partners))

    started = []

    def send(src, dst, send_sem, recv_sem, target):
        copy = pltpu.make_async_remote_copy(
            src_ref=src, dst_ref=dst, send_sem=send_sem, recv_sem=recv_sem,
            device_id={"row": target}, device_id_type=MESH)
        copy.start()
        started.append(copy)
        return copy

    def divide(slot, high_ref, low_ref):
        chunk = min(64, size)

        def part(step, carry):
            rows = pl.ds(pl.multiple_of(step * chunk, chunk), chunk)
            high, low = split(stage[slot, rows, :])
            high_ref[slot, rows, :] = high
            low_ref[slot, rows, :] = low
            return carry

        lax.fori_loop(0, size // chunk, part, 0)

    def gather_apply(phase, own, high_ref, low_ref, loads, after):
        copies = {}

        def give(src, key, target):
            slot = slot_of(*key)
            copies[key] = send(src, gathered.at[phase, slot], gather_send.at[phase, slot],
                               gather_recv.at[phase, slot], target)

        give(own, (0, 0, 1), at(0, 0, 1))
        give(own, (0, 1, 0), at(0, 1, 0))
        for dz in range(1, lines):
            give(own, (dz, 0, 0), at(lines - dz, 0, 0))
        total = None
        for key in slots:
            dz, dy, dc = key
            slot = slot_of(*key)
            block = own
            if slot:
                copies[key].wait_recv()
                block = gathered.at[phase, slot]
                if dc == 0:
                    if dy == 0:
                        give(block, (dz, 1, 0), at(0, 1, 0))
                    give(block, (dz, dy, 1), at(0, 0, 1))
            loads[slot].wait()
            divide(slot, high_ref, low_ref)
            after(key)
            both, high = stacked(block[...])
            term = product(both, high, high_ref[slot], low_ref[slot], NT)
            total = term if total is None else total + term
        return total

    def scatter_apply(phase, value, high_ref, low_ref):
        both, high = stacked(value)

        def part(dz, dy, dc):
            slot = slot_of(dz, dy, dc)
            return product(both, high, high_ref[slot], low_ref[slot], NN)

        def to_core(dz, dy):
            slot = dz * sides + dy
            core_out[phase, slot] = part(dz, dy, 1)
            return send(core_out.at[phase, slot], core_in.at[phase, slot], core_send.at[phase, slot],
                        core_recv.at[phase, slot], at(0, 0, 1))

        side_copies, line_copies = {}, {}

        def finish(dz):
            side_copies[dz].wait_recv()
            line_out[phase, dz] = line_out[phase, dz] + side_in[phase, dz]
            line_copies[dz] = send(line_out.at[phase, dz], line_in.at[phase, dz], line_send.at[phase, dz],
                                   line_recv.at[phase, dz], at(dz, 0, 0))

        pending = None
        for dz in list(range(1, lines)) + [0]:
            other = to_core(dz, 1)
            same = to_core(dz, 0)
            mine = part(dz, 1, 0)
            other.wait_recv()
            side_out[phase, dz] = mine + core_in[phase, dz * sides + 1]
            side_copies[dz] = send(side_out.at[phase, dz], side_in.at[phase, dz], side_send.at[phase, dz],
                                   side_recv.at[phase, dz], at(0, 1, 0))
            mine = part(dz, 0, 0)
            if pending is not None:
                finish(pending)
            same.wait_recv()
            line_out[phase, dz] = mine + core_in[phase, dz * sides]
            pending = dz
        side_copies[0].wait_recv()
        total = line_out[phase, 0] + side_in[phase, 0]
        for dz in range(1, lines):
            line_copies[dz].wait_recv()
            total = total + line_in[phase, dz]
        return total

    lower_loads = {}

    def load_lower(key):
        lower_loads[slot_of(*key)] = load(lower_hbm, 1, key)

    down_ref[...] = gather_apply(0, source_ref, upper_high, upper_low, upper_loads, load_lower)
    field = gather_apply(1, down_ref, lower_high, lower_low, lower_loads, lambda key: None)
    field_ref[...] = field
    scaled = lower_gain[...] * field + inside_ref[...]
    bounced = scatter_apply(0, scaled, lower_high, lower_low)
    mixed = upper_gain[...] * bounced - down_ref[...]
    reflected_ref[...] = scatter_apply(1, mixed, upper_high, upper_low)
    for copy in started:
        copy.wait_send()


def body(devices, sources, lower_sources, upper_operator, lower_operator, upper_impedance, lower_impedance):
    batch_count, column_count, size = sources.shape
    columns = batch_count * column_count
    cores, sides = 2, 2
    lines = devices // (cores * sides)
    vmem, dma = pltpu.VMEM, pltpu.SemaphoreType.DMA
    traces = jax.ShapeDtypeStruct((columns, size), F32)
    whole = pl.BlockSpec(memory_space=pltpu.VMEM)
    remote = pl.BlockSpec(memory_space=pl.ANY)
    field, reflected = pl.pallas_call(
        functools.partial(kernel, lines, sides, cores),
        out_shape=(traces, traces),
        in_specs=[whole, whole, remote, remote, whole, whole],
        out_specs=(whole, whole),
        scratch_shapes=[
            vmem((devices, size, size), F32),
            vmem((devices, size, size), BF16),
            vmem((devices, size, size), BF16),
            vmem((devices, size, size), BF16),
            vmem((devices, size, size), BF16),
            vmem((2, devices, columns, size), F32),
            vmem((columns, size), F32),
            vmem((2, lines * sides, columns, size), F32),
            vmem((2, lines * sides, columns, size), F32),
            vmem((2, lines, columns, size), F32),
            vmem((2, lines, columns, size), F32),
            vmem((2, lines, columns, size), F32),
            vmem((2, lines, columns, size), F32),
            dma((2, devices)),
            dma((2, devices)),
            dma((2, devices)),
            dma((2, lines * sides)),
            dma((2, lines * sides)),
            dma((2, lines)),
            dma((2, lines)),
            dma((2, lines)),
            dma((2, lines)),
        ],
        compiler_params=pltpu.CompilerParams(
            collective_id=0, has_side_effects=True, vmem_limit_bytes=60 * 1024 * 1024),
    )(
        sources.reshape(columns, size),
        lower_sources.reshape(columns, size),
        upper_operator,
        lower_operator,
        upper_impedance.reshape(1, size),
        lower_impedance.reshape(1, size),
    )
    shape = (batch_count, column_count, size)
    return field.reshape(shape), reflected.reshape(shape)


def solution(mesh):
    placed = (
        P("group", None, "row"),
        P("group", None, "row"),
        P(("group", "row"), None),
        P(("group", "row"), None),
        P(("group", "row")),
        P(("group", "row")),
    )
    return jax.shard_map(
        functools.partial(body, mesh.shape["row"]),
        mesh=mesh,
        in_specs=placed,
        out_specs=(P("group", None, "row"), P("group", None, "row")),
        check_vma=False,
    )
```

```python
import functools

import jax
import jax.numpy as jnp
from jax import lax
from jax.experimental import pallas as pl
from jax.experimental.pallas import tpu as pltpu
from jax.sharding import PartitionSpec as P

MESH = pl.DeviceIdType.MESH
F32, BF16 = jnp.float32, jnp.bfloat16
NT = (((1,), (1,)), ((), ()))
NN = (((1,), (0,)), ((), ()))


def split(value):
    high = value.astype(BF16)
    return high, (value - high.astype(F32)).astype(BF16)


def stacked(value):
    high, low = split(value)
    return jnp.concatenate([high, low], axis=0), high


def folded(value):
    rows = value.shape[0] // 2
    return value[:rows] + value[rows:]


def kernel(lines, sides, cores, source_ref, inside_ref, upper_hbm, lower_hbm, upper_gain, lower_gain,
           field_ref, reflected_ref,
           stage, upper, lower, gathered, down_ref, sums,
           core_out, core_in, side_out, side_in, line_out, line_in,
           load_sem, gather_send, gather_recv, core_send, core_recv, side_send, side_recv, line_send, line_recv):
    size = source_ref.shape[1]
    me = lax.axis_index("row")
    core = lax.rem(me, cores)
    side = lax.rem(me // cores, sides)
    line = me // (cores * sides)

    def at(dz, dy, dc):
        return (lax.rem(line + dz, lines) * sides + lax.rem(side + dy, sides)) * cores + lax.rem(core + dc, cores)

    def slot_of(dz, dy, dc):
        return (dz * sides + dy) * cores + dc

    slots = [(dz, dy, dc) for dz in range(lines) for dy in range(sides) for dc in range(cores)]

    def load(operator, which, key):
        slot = slot_of(*key)
        columns = pl.ds(pl.multiple_of(at(*key) * size, size), size)
        copy = pltpu.make_async_copy(operator.at[:, columns], stage.at[slot], load_sem.at[which, slot])
        copy.start()
        return copy

    upper_loads = [load(upper_hbm, 0, key) for key in slots]

    partners = [at(0, 0, 1), at(0, 1, 0)] + [at(dz, 0, 0) for dz in range(1, lines)]
    barrier = pltpu.get_barrier_semaphore()
    for partner in partners:
        pl.semaphore_signal(barrier, inc=1, device_id={"row": partner}, device_id_type=MESH)
    pl.semaphore_wait(barrier, len(partners))

    started = []

    def send(src, dst, send_sem, recv_sem, target):
        copy = pltpu.make_async_remote_copy(
            src_ref=src, dst_ref=dst, send_sem=send_sem, recv_sem=recv_sem,
            device_id={"row": target}, device_id_type=MESH)
        copy.start()
        started.append(copy)
        return copy

    def gather_apply(phase, own, parts, loads, after):
        copies = {}
        chunk = min(256, size)

        def give(src, key, target):
            slot = slot_of(*key)
            copies[key] = send(src, gathered.at[phase, slot], gather_send.at[phase, slot],
                               gather_recv.at[phase, slot], target)

        def arrive(key):
            dz, dy, dc = key
            slot = slot_of(*key)
            copies[key].wait_recv()
            if dc == 0:
                if dy == 0:
                    give(gathered.at[phase, slot], (dz, 1, 0), at(0, 1, 0))
                give(gathered.at[phase, slot], (dz, dy, 1), at(0, 0, 1))

        def add(keys):
            for key in keys:
                loads[slot_of(*key)].wait()
            for key in keys:
                slot = slot_of(*key)
                both = stacked(gathered[phase, slot] if slot else own[...])[0]
                for begin in range(0, size, chunk):
                    high, low = split(stage[slot, begin:begin + chunk, :])
                    parts[slot, begin:begin + chunk, :] = high
                    parts[slot, size + begin:size + begin + chunk, :] = low
                    term = folded(lax.dot_general(
                        jnp.concatenate([high, low], axis=0), both, NT, preferred_element_type=F32))
                    if slot:
                        sums[begin:begin + chunk, :] += term
                    else:
                        sums[begin:begin + chunk, :] = term
            for key in keys:
                after(key)

        for dz in range(1, lines):
            give(own, (dz, 0, 0), at(lines - dz, 0, 0))
        give(own, (0, 1, 0), at(0, 1, 0))
        give(own, (0, 0, 1), at(0, 0, 1))
        add([(0, 0, 0)])
        late = (0, 0, 1)
        for dz in range(lines):
            for dy in range(sides):
                if dz or dy:
                    arrive((dz, dy, 0))
                    arrive(late)
                    add([(dz, dy, 0), late])
                    late = (dz, dy, 1)
        arrive(late)
        add([late])
        return folded(sums[...].T)

    def scatter_apply(phase, value, parts):
        both = stacked(value)[0]
        both = jnp.concatenate([both, both], axis=1)

        def part(dz, dy, dc):
            return folded(lax.dot_general(both, parts[slot_of(dz, dy, dc)], NN, preferred_element_type=F32))

        core_copies, side_copies, line_copies = {}, {}, {}

        def compute(dz, dy):
            slot = dz * sides + dy
            other = part(dz, dy, 1)
            mine = part(dz, dy, 0)
            core_out[phase, slot] = other
            core_copies[dz, dy] = send(
                core_out.at[phase, slot], core_in.at[phase, slot], core_send.at[phase, slot],
                core_recv.at[phase, slot], at(0, 0, 1))
            (side_out if dy else line_out)[phase, dz] = mine

        def merge(dz, dy):
            out = side_out if dy else line_out
            core_copies[dz, dy].wait_recv()
            out[phase, dz] = out[phase, dz] + core_in[phase, dz * sides + dy]
            if dy:
                side_copies[dz] = send(side_out.at[phase, dz], side_in.at[phase, dz], side_send.at[phase, dz],
                                       side_recv.at[phase, dz], at(0, 1, 0))

        def finish(dz):
            side_copies[dz].wait_recv()
            line_out[phase, dz] = line_out[phase, dz] + side_in[phase, dz]
            if dz:
                line_copies[dz] = send(line_out.at[phase, dz], line_in.at[phase, dz], line_send.at[phase, dz],
                                       line_recv.at[phase, dz], at(dz, 0, 0))

        far = list(range(1, lines)) + [0]
        order = [(far[0], 1)]
        for before, now in zip(far, far[1:]):
            order += [(now, 1), (before, 0)]
        order += [(0, 0)]
        merged = []
        for step, key in enumerate(order):
            compute(*key)
            if merged:
                finish(merged.pop())
            if step:
                merge(*order[step - 1])
                if order[step - 1][1] == 0:
                    merged.append(order[step - 1][0])
        for dz in merged:
            finish(dz)
        merge(*order[-1])
        finish(0)
        total = line_out[phase, 0]
        for dz in range(1, lines):
            line_copies[dz].wait_recv()
            total = total + line_in[phase, dz]
        return total

    lower_loads = {}

    def load_lower(key):
        lower_loads[slot_of(*key)] = load(lower_hbm, 1, key)

    down_ref[...] = gather_apply(0, source_ref, upper, upper_loads, load_lower)
    field = gather_apply(1, down_ref, lower, lower_loads, lambda key: None)
    field_ref[...] = field
    scaled = lower_gain[...] * field + inside_ref[...]
    bounced = scatter_apply(0, scaled, lower)
    mixed = upper_gain[...] * bounced - down_ref[...]
    reflected_ref[...] = scatter_apply(1, mixed, upper)
    for copy in started:
        copy.wait_send()


def write(field_in, reflected_in, field_out, reflected_out, sems):
    first = pltpu.make_async_copy(field_in, field_out, sems.at[0])
    second = pltpu.make_async_copy(reflected_in, reflected_out, sems.at[1])
    first.start()
    second.start()
    first.wait()
    second.wait()


def body(devices, sources, lower_sources, upper_operator, lower_operator, upper_impedance, lower_impedance):
    batch_count, column_count, size = sources.shape
    columns = batch_count * column_count
    cores, sides = 2, 2
    lines = devices // (cores * sides)
    vmem, dma = pltpu.VMEM, pltpu.SemaphoreType.DMA
    traces = jax.ShapeDtypeStruct((columns, size), F32)
    whole = pl.BlockSpec(memory_space=pltpu.VMEM)
    remote = pl.BlockSpec(memory_space=pl.ANY)
    field, reflected = pl.pallas_call(
        functools.partial(kernel, lines, sides, cores),
        out_shape=(traces, traces),
        in_specs=[whole, whole, remote, remote, whole, whole],
        out_specs=(whole, whole),
        scratch_shapes=[
            vmem((devices, size, size), F32),
            vmem((devices, 2 * size, size), BF16),
            vmem((devices, 2 * size, size), BF16),
            vmem((2, devices, columns, size), F32),
            vmem((columns, size), F32),
            vmem((size, 2 * columns), F32),
            vmem((2, lines * sides, columns, size), F32),
            vmem((2, lines * sides, columns, size), F32),
            vmem((2, lines, columns, size), F32),
            vmem((2, lines, columns, size), F32),
            vmem((2, lines, columns, size), F32),
            vmem((2, lines, columns, size), F32),
            dma((2, devices)),
            dma((2, devices)),
            dma((2, devices)),
            dma((2, lines * sides)),
            dma((2, lines * sides)),
            dma((2, lines)),
            dma((2, lines)),
            dma((2, lines)),
            dma((2, lines)),
        ],
        compiler_params=pltpu.CompilerParams(
            collective_id=0, has_side_effects=True, vmem_limit_bytes=60 * 1024 * 1024),
    )(
        sources.reshape(columns, size),
        lower_sources.reshape(columns, size),
        upper_operator,
        lower_operator,
        upper_impedance.reshape(1, size),
        lower_impedance.reshape(1, size),
    )
    field, reflected = pl.pallas_call(
        write,
        out_shape=(traces, traces),
        in_specs=[remote, remote],
        out_specs=(remote, remote),
        scratch_shapes=[dma((2,))],
    )(field, reflected)
    shape = (batch_count, column_count, size)
    return field.reshape(shape), reflected.reshape(shape)


def solution(mesh):
    placed = (
        P("group", None, "row"),
        P("group", None, "row"),
        P(("group", "row"), None),
        P(("group", "row"), None),
        P(("group", "row")),
        P(("group", "row")),
    )
    return jax.shard_map(
        functools.partial(body, mesh.shape["row"]),
        mesh=mesh,
        in_specs=placed,
        out_specs=(P("group", None, "row"), P("group", None, "row")),
        check_vma=False,
    )
```

```python
import functools

import jax
import jax.numpy as jnp
from jax import lax
from jax.experimental import pallas as pl
from jax.experimental.pallas import tpu as pltpu
from jax.sharding import PartitionSpec as P

MESH = pl.DeviceIdType.MESH
F32, BF16 = jnp.float32, jnp.bfloat16
NT = (((1,), (1,)), ((), ()))
NN = (((1,), (0,)), ((), ()))


def split(value):
    high = value.astype(BF16)
    return high, (value - high.astype(F32)).astype(BF16)


def stacked(value):
    return jnp.concatenate(split(value), axis=0)


def folded(value):
    rows = value.shape[0] // 2
    return value[:rows] + value[rows:]


def kernel(chips, sides, cores, source_ref, inside_ref, upper_hbm, lower_hbm, upper_gain, lower_gain,
           field_ref, reflected_ref,
           stage, upper, lower, gathered, down_ref, sums, core_out, core_in, work, ring_in,
           load_sem, core_send, core_recv, ring_send, ring_recv, pair_send, pair_recv, pass_send, pass_recv):
    columns, size = source_ref.shape
    lines, half = chips // sides, columns // 2
    middle = chips // 2
    me = lax.axis_index("row")
    core = lax.rem(me, cores)
    side = lax.rem(me // cores, sides)
    line = me // (cores * sides)
    place = side * (chips - 1 - line) + (1 - side) * line

    def at(hops, dc):
        there = lax.rem(place + hops + chips, chips)
        turned = there // lines
        row = turned * (chips - 1 - there) + (1 - turned) * there
        return (row * sides + turned) * cores + lax.rem(core + dc, cores)

    def slot_of(k, dc):
        return k * cores + dc

    def rows(chunk):
        return pl.ds(chunk * half, half)

    def reach(way, chunk):
        return middle if way == chunk else chips - 1 - middle

    pairs = [(way, chunk) for chunk in range(2) for way in range(2)]
    step_of = (1, -1)
    visit = [0]
    for near in range(1, middle):
        visit += [near, chips - near]
    visit += [middle]

    def load(operator, which, k, dc):
        slot = slot_of(k, dc)
        wanted = pl.ds(pl.multiple_of(at(-k, dc) * size, size), size)
        copy = pltpu.make_async_copy(operator.at[:, wanted], stage.at[slot], load_sem.at[which, slot])
        copy.start()
        return copy

    upper_loads = {slot_of(k, dc): load(upper_hbm, 0, k, dc) for k in visit for dc in range(cores)}

    partners = [at(0, 1), at(1, 0), at(-1, 0)]
    barrier = pltpu.get_barrier_semaphore()
    for partner in partners:
        pl.semaphore_signal(barrier, inc=1, device_id={"row": partner}, device_id_type=MESH)
    pl.semaphore_wait(barrier, len(partners))

    started = []

    def send(src, dst, send_sem, recv_sem, target):
        copy = pltpu.make_async_remote_copy(
            src_ref=src, dst_ref=dst, send_sem=send_sem, recv_sem=recv_sem,
            device_id={"row": target}, device_id_type=MESH)
        copy.start()
        started.append(copy)
        return copy

    def gather_apply(phase, own, parts, loads, after):
        ring, pair = {}, {}
        chunk_rows = min(256, size)

        def hop(way, chunk, distance):
            k = distance if way == 0 else chips - distance
            before = k - 1 if way == 0 else (k + 1) % chips
            src = own if distance == 1 else gathered.at[phase, slot_of(before, 0)]
            ring[way, chunk, distance] = send(
                src.at[rows(chunk)], gathered.at[phase, slot_of(k, 0), rows(chunk)],
                ring_send.at[phase, k, chunk], ring_recv.at[phase, k, chunk], at(step_of[way], 0))

        def share(k):
            src = gathered.at[phase, slot_of(k, 0)] if k else own
            pair[k] = send(src, gathered.at[phase, slot_of(k, 1)], pair_send.at[phase, k],
                           pair_recv.at[phase, k], at(0, 1))

        groups = [[(0, 0)], [(0, 1)]]
        for distance in range(1, middle + 1):
            here = sorted({distance, chips - distance})
            groups += [[(k, dc) for k in here] for dc in range(cores)]

        def divide(k, dc):
            slot = slot_of(k, dc)
            for begin in range(0, size, chunk_rows):
                high, low = split(stage[slot, begin:begin + chunk_rows, :])
                parts[slot, begin:begin + chunk_rows, :] = high
                parts[slot, size + begin:size + begin + chunk_rows, :] = low

        def add(keys):
            following = groups[groups.index(keys) + 1] if keys != groups[-1] else []
            for k, dc in keys:
                if dc:
                    pair[k].wait_recv()
            for key in following:
                loads[slot_of(*key)].wait()
            total = None
            for place_of, (k, dc) in enumerate(keys):
                slot = slot_of(k, dc)
                if place_of < len(following):
                    divide(*following[place_of])
                both = stacked(gathered[phase, slot] if slot else own[...])
                term = folded(lax.dot_general(parts[slot], both, NT, preferred_element_type=F32))
                total = term if total is None else total + term
            for key in following[len(keys):]:
                divide(*key)
            if keys == groups[0]:
                sums[...] = total
            else:
                sums[...] += total
            for key in following:
                after(*key)

        for way, chunk in pairs:
            hop(way, chunk, 1)
        share(0)
        loads[0].wait()
        divide(0, 0)
        after(0, 0)
        add([(0, 0)])
        late = [(0, 1)]
        for distance in range(1, middle + 1):
            here = sorted({distance, chips - distance})
            for way, chunk in pairs:
                if chunk == 1 and way == 0 and late:
                    add(late)
                    late = []
                if distance <= reach(way, chunk):
                    ring[way, chunk, distance].wait_recv()
                    if distance < reach(way, chunk):
                        hop(way, chunk, distance + 1)
            for k in here:
                share(k)
            add([(k, 0) for k in here])
            late = [(k, 1) for k in here]
        add(late)
        return folded(sums[...].T)

    def scatter_apply(phase, value, parts):
        both = stacked(value)
        both = jnp.concatenate([both, both], axis=1)

        def part(k, dc):
            return folded(lax.dot_general(both, parts[slot_of(k, dc)], NN, preferred_element_type=F32))

        pair, ring = {}, {}

        def compute(keys):
            others = [part(k, 1) for k in keys]
            for k, other in zip(keys, others):
                core_out[phase, k] = other
                pair[k] = send(core_out.at[phase, k], core_in.at[phase, k], core_send.at[phase, k],
                               core_recv.at[phase, k], at(0, 1))
            for k in keys:
                work[phase, k] = part(k, 0)

        def pass_on(distance):
            for k in sorted({distance, chips - distance}):
                pair[k].wait_recv()
                work[phase, k] = work[phase, k] + core_in[phase, k]
            for way, chunk in pairs:
                if distance > reach(way, chunk):
                    continue
                k = chips - distance if way == 0 else distance
                if distance < reach(way, chunk):
                    ring[way, chunk, distance].wait_recv()
                    work[phase, k, rows(chunk)] = work[phase, k, rows(chunk)] + ring_in[phase, way, distance, rows(chunk)]
                ring[way, chunk, distance - 1] = send(
                    work.at[phase, k, rows(chunk)], ring_in.at[phase, way, distance - 1, rows(chunk)],
                    pass_send.at[phase, way, distance - 1, chunk], pass_recv.at[phase, way, distance - 1, chunk],
                    at(step_of[way], 0))

        compute([middle])
        for distance in range(middle - 1, -1, -1):
            compute(sorted({distance, (chips - distance) % chips}))
            pass_on(distance + 1)
        pair[0].wait_recv()
        total = work[phase, 0] + core_in[phase, 0]
        for way, chunk in pairs:
            ring[way, chunk, 0].wait_recv()
        return total + ring_in[phase, 0, 0] + ring_in[phase, 1, 0]

    lower_loads = {}

    def load_lower(k, dc):
        lower_loads[slot_of(k, dc)] = load(lower_hbm, 1, k, dc)

    down_ref[...] = gather_apply(0, source_ref, upper, upper_loads, load_lower)
    field = gather_apply(1, down_ref, lower, lower_loads, lambda k, dc: None)
    field_ref[...] = field
    scaled = lower_gain[...] * field + inside_ref[...]
    bounced = scatter_apply(0, scaled, lower)
    mixed = upper_gain[...] * bounced - down_ref[...]
    reflected_ref[...] = scatter_apply(1, mixed, upper)
    for copy in started:
        copy.wait_send()


def body(devices, sources, lower_sources, upper_operator, lower_operator, upper_impedance, lower_impedance):
    batch_count, column_count, size = sources.shape
    columns = batch_count * column_count
    cores, sides = 2, 2
    chips = devices // cores
    middle = chips // 2
    vmem, dma = pltpu.VMEM, pltpu.SemaphoreType.DMA
    traces = jax.ShapeDtypeStruct((columns, size), F32)
    whole = pl.BlockSpec(memory_space=pltpu.VMEM)
    remote = pl.BlockSpec(memory_space=pl.ANY)
    field, reflected = pl.pallas_call(
        functools.partial(kernel, chips, sides, cores),
        out_shape=(traces, traces),
        in_specs=[whole, whole, remote, remote, whole, whole],
        out_specs=(whole, whole),
        scratch_shapes=[
            vmem((devices, size, size), F32),
            vmem((devices, 2 * size, size), BF16),
            vmem((devices, 2 * size, size), BF16),
            vmem((2, devices, columns, size), F32),
            vmem((columns, size), F32),
            vmem((size, 2 * columns), F32),
            vmem((2, chips, columns, size), F32),
            vmem((2, chips, columns, size), F32),
            vmem((2, chips, columns, size), F32),
            vmem((2, 2, middle, columns, size), F32),
            dma((2, devices)),
            dma((2, chips)),
            dma((2, chips)),
            dma((2, chips, 2)),
            dma((2, chips, 2)),
            dma((2, chips)),
            dma((2, chips)),
            dma((2, 2, middle, 2)),
            dma((2, 2, middle, 2)),
        ],
        compiler_params=pltpu.CompilerParams(
            collective_id=0, has_side_effects=True, vmem_limit_bytes=60 * 1024 * 1024),
    )(
        sources.reshape(columns, size),
        lower_sources.reshape(columns, size),
        upper_operator,
        lower_operator,
        upper_impedance.reshape(1, size),
        lower_impedance.reshape(1, size),
    )
    shape = (batch_count, column_count, size)
    return field.reshape(shape), reflected.reshape(shape)


def solution(mesh):
    placed = (
        P("group", None, "row"),
        P("group", None, "row"),
        P(("group", "row"), None),
        P(("group", "row"), None),
        P(("group", "row")),
        P(("group", "row")),
    )
    return jax.shard_map(
        functools.partial(body, mesh.shape["row"]),
        mesh=mesh,
        in_specs=placed,
        out_specs=(P("group", None, "row"), P("group", None, "row")),
        check_vma=False,
    )
```
